512 devices in a mesh: blk: 32 (over x, y, core), tile: 16 (over z).
Axes of the slice: x: 4, y: 4, z: 16, core: 2. Of those that a mesh axis runs over, the one named last changes fastest.
Arguments:
- field: bfloat16 [32, 16, 1024, 128], P('blk', 'tile'), may hold values from -6 to 6
- grid_cotangent: bfloat16 [32, 16, 2048, 128], P('blk', 'tile'), may hold values from -6 to 6
- send_rows: int32 [32, 16, 4, 256], P('blk', 'tile'), may hold values from 0 to 1023
- neighbors: int32 [32, 16, 1024, 8], P('blk', 'tile'), may hold values from 0 to 2047
- stencil: float32 [32, 16, 1024, 8], P('blk', 'tile'), may hold values from -2.5 to 2.5
- vertical: float32 [2, 16, 16], replicated, may hold values from -1.5 to 1.5
- interp_weights: bfloat16 [32, 16, 16, 128, 128], P('blk', 'tile'), may hold values from -0.5 to 0.5
- block_map: int32 [32, 16, 16, 128], P('blk', 'tile'), may hold values from 0 to 1023
- live_block_tally: int32 [32, 16], P('blk', 'tile'), may hold values from 2 to 16, as said below
Outputs:
- grid_field: bfloat16 [32, 16, 2048, 128], P('blk', 'tile')
- subgrid_gradient: bfloat16 [32, 16, 1024, 128], P('blk', 'tile')
The draws below stay inside these ranges and needn't reach their ends.
Inputs may be any that keep to these rules, and one draw needn't show every extreme that they name: `live_block_tally`: each device's count is one of 16, 8, 4, 2; at least one device has 16.
All inputs are finite; a program needn't handle non-finite values.
Results may differ from the reference program's by a relative error of at most 0.017.
Values may be sent and summed in bfloat16 or wider, within the bound.
No kernel may reach another device: no remote copies, remote signals or barrier semaphores. Data moves between devices by JAX's collectives and lax.ppermute only.
A program may use at most 64 MiB of HBM per device.

```python
import jax
import jax.numpy as jnp
from jax import lax

MEMBERS = 4
VARS = 2
LEV = 16
R = 1024
K = 8
BLOCK = 128
H = 256
NB_MAX = 16
F = 128
N_BLK = 32
N_TILE = 16


def draw_live_block_tally(key, part):
    key = jax.random.fold_in(key, 7)
    first, second = jax.random.split(key)
    powers = jax.random.randint(first, (N_BLK, N_TILE), 0, 4)
    counts = NB_MAX // jnp.power(2, powers)
    chosen = jax.random.randint(second, (), 0, N_BLK * N_TILE)
    positions = jnp.arange(N_BLK * N_TILE, dtype=jnp.int32).reshape(N_BLK, N_TILE)
    return jnp.where(positions == chosen, NB_MAX, counts).astype(jnp.int32)


def place_ends(entries, own_key, low, top_value):
    extent = entries.shape
    index_at = [jax.random.randint(jax.random.fold_in(own_key, axis), (), 0, extent[axis]) for axis in range(len(extent))]
    entries = entries.at[tuple(index_at)].set(low)
    longest = extent.index(max(extent))
    index_at[longest] = (index_at[longest] + 1) % extent[longest]
    return entries.at[tuple(index_at)].set(top_value)


def level_of(rng, shape, cuts, smallest, top_value):
    def one(dim, blocks):
        draws = jax.random.uniform(jax.random.fold_in(jax.random.fold_in(rng, 6), dim), (blocks,), jnp.float32, smallest / len(cuts), top_value / len(cuts))
        return jnp.repeat(jnp.exp(draws), shape[dim] // blocks).reshape((-1,) + (1,) * (len(shape) - dim - 1))

    gain = one(*cuts[0])
    for cut in cuts[1:]:
        gain = gain * one(*cut)
    return gain


def scatter_about(own_key, extent, scale, bound, shards=(), kind=jnp.bfloat16):
    result = jax.random.normal(own_key, extent, jnp.float32) * scale
    if len(shards) > 0:
        result = level_of(own_key, extent, shards, -0.22, 0.18) * result
    return jnp.clip(result, min=-bound, max=bound).astype(kind)


def setup_inputs(seed: int = 0) -> dict:
    keys = jax.random.split(jax.random.key(seed), 10)
    field = scatter_about(keys[0], (N_BLK, N_TILE, R, F), 1.0, 6.0, ((0, 32), (1, 16)))
    grid_cotangent = scatter_about(keys[1], (N_BLK, N_TILE, NB_MAX * BLOCK, F), 1.0, 6.0, ((0, 32), (1, 16)))
    send_rows = place_ends(jax.random.randint(keys[2], (N_BLK, N_TILE, 4, H), 0, R), jax.random.fold_in(keys[2], 1), 0, R - 1).astype(jnp.int32)
    neighbors = place_ends(jax.random.randint(keys[3], (N_BLK, N_TILE, R, K), 0, R + 4 * H), jax.random.fold_in(keys[3], 1), 0, (R + 4 * H) - 1).astype(jnp.int32)
    stencil = scatter_about(keys[4], (N_BLK, N_TILE, R, K), 0.35, 2.5, ((0, 32), (1, 16)), jnp.float32)
    vertical = scatter_about(keys[5], (VARS, LEV, LEV), LEV ** -0.5, 1.5, (), jnp.float32)
    interp_weights = scatter_about(keys[6], (N_BLK, N_TILE, NB_MAX, BLOCK, BLOCK), BLOCK ** -0.5, 0.5, ((0, 32), (1, 16)))
    block_map = place_ends(jax.random.randint(keys[7], (N_BLK, N_TILE, NB_MAX, BLOCK), 0, R), jax.random.fold_in(keys[7], 1), 0, R - 1).astype(jnp.int32)
    live_block_tally = draw_live_block_tally(jax.random.fold_in(keys[9], 71), 0)
    return dict(field=field, grid_cotangent=grid_cotangent, send_rows=send_rows, neighbors=neighbors, stencil=stencil, vertical=vertical, interp_weights=interp_weights, block_map=block_map, live_block_tally=live_block_tally)


def level_matrix(vertical, member_list):
    variable_count = vertical.shape[0]
    level_count = vertical.shape[1]
    member_identity = jnp.eye(member_list, dtype=jnp.float32)
    variable_identity = jnp.eye(variable_count, dtype=jnp.float32)
    block_stack = jnp.einsum('ec,yf,yhs->eyhcfs', member_identity, variable_identity, vertical.astype(jnp.float32))
    width = member_list * variable_count * level_count
    return block_stack.reshape(width, width)


def take_rows(values, indices):
    return jax.vmap(jax.vmap(lambda table, rows: table[rows]))(values, indices)


def from_lower_tile(pieces):
    return jnp.concatenate([jnp.zeros_like(pieces[:, :1]), pieces[:, :-1]], axis=1)


def from_upper_tile(pieces):
    return jnp.concatenate([pieces[:, 1:], jnp.zeros_like(pieces[:, :1])], axis=1)


def add_rows(total, rows, extra):
    return total.at[rows].add(extra.astype(jnp.float32))


def reference(field, grid_cotangent, send_rows, neighbors, stencil, vertical, interp_weights, block_map, live_block_tally):
    mixing = level_matrix(vertical, MEMBERS)
    outgoing = [take_rows(field, send_rows[:, :, q]) for q in range(4)]
    incoming = [jnp.roll(outgoing[0], 1, axis=0), jnp.roll(outgoing[1], -1, axis=0),
                from_lower_tile(outgoing[2]), from_upper_tile(outgoing[3])]
    extended = jnp.concatenate([field] + incoming, axis=2)
    device_total = N_BLK * N_TILE

    def flatten_rows(values):
        return values.reshape((device_total,) + values.shape[2:])

    def device_work(items):
        ext_rows, adjacent, coeffs, weight_table, block_rows, live_count, cotangent = items
        feat = ext_rows.shape[1]
        horizontal = jnp.zeros((R, feat), jnp.float32)
        for k in range(K):
            horizontal = horizontal + coeffs[:, k:k + 1] * ext_rows[adjacent[:, k]].astype(jnp.float32)
        converted = jnp.dot(horizontal, mixing, precision=lax.Precision.HIGHEST,
                            preferred_element_type=jnp.float32).astype(jnp.bfloat16)
        live = (jnp.arange(NB_MAX) < live_count)[:, None, None]
        source = converted[block_rows]
        grid = jnp.einsum('jrs,jsf->jrf', weight_table.astype(jnp.float32), source.astype(jnp.float32))
        grid = jnp.where(live, grid, 0.0).astype(jnp.bfloat16).reshape(NB_MAX * BLOCK, feat)
        cot_blocks = jnp.where(live, cotangent.reshape(NB_MAX, BLOCK, feat).astype(jnp.float32), 0.0)
        back_blocks = jnp.einsum('jrs,jrf->jsf', weight_table.astype(jnp.float32), cot_blocks)
        back = jax.ops.segment_sum(back_blocks.reshape(NB_MAX * BLOCK, feat), block_rows.reshape(-1), num_segments=R)
        mixed_back = jnp.dot(back, mixing.T, precision=lax.Precision.HIGHEST, preferred_element_type=jnp.float32)
        adjoint_extended = jnp.zeros((R + 4 * H, feat), jnp.float32)
        for k in range(K):
            adjoint_extended = adjoint_extended.at[adjacent[:, k]].add(coeffs[:, k:k + 1] * mixed_back)
        halo_back = adjoint_extended[R:].astype(jnp.bfloat16).reshape(4, H, feat)
        return grid, adjoint_extended[:R], halo_back

    grid, local_part, halo_back = lax.map(device_work, (
        flatten_rows(extended), flatten_rows(neighbors), flatten_rows(stencil), flatten_rows(interp_weights),
        flatten_rows(block_map), flatten_rows(live_block_tally), flatten_rows(grid_cotangent)))
    grid = grid.reshape((N_BLK, N_TILE) + grid.shape[1:])
    gradient = local_part.reshape((N_BLK, N_TILE) + local_part.shape[1:])
    halo_back = halo_back.reshape((N_BLK, N_TILE) + halo_back.shape[1:])
    returned = [jnp.roll(halo_back[:, :, 0], -1, axis=0), jnp.roll(halo_back[:, :, 1], 1, axis=0),
                from_upper_tile(halo_back[:, :, 2]), from_lower_tile(halo_back[:, :, 3])]
    for q in range(4):
        gradient = jax.vmap(jax.vmap(add_rows))(gradient, send_rows[:, :, q], returned[q])
    return grid, gradient.astype(jnp.bfloat16)
```

```python
import jax
import jax.numpy as jnp
from jax import lax
from jax.experimental import pallas as pl
from jax.experimental.pallas import tpu as pltpu
from jax.sharding import PartitionSpec as P

MEMBERS = 4
LANES = 128
GROUP = 16
BF16 = jnp.bfloat16
F32 = jnp.float32
I32 = jnp.int32
VMEM_LIMIT = 56 * 1024 * 1024


def iota(shape, dim):
    return lax.broadcasted_iota(I32, shape, dim)


def dot(left, right, left_dim=1, right_dim=0):
    return lax.dot_general(
        left, right, (((left_dim,), (right_dim,)), ((), ())), preferred_element_type=F32
    )


def neighbor_order():
    blk_odd = lax.rem(lax.axis_index("blk"), 2)
    tile_odd = lax.rem(lax.axis_index("tile"), 2)
    return (blk_odd, 1 - blk_odd, 2 + tile_odd, 3 - tile_odd)


def mixing_matrix(vert_ref):
    rows, levels = vert_ref.shape
    tall = jnp.concatenate([vert_ref[...].astype(BF16)] * MEMBERS, axis=0)
    feat = tall.shape[0]
    repeat = jnp.where(
        lax.rem(iota((levels, feat), 1), levels) == iota((levels, feat), 0), 1.0, 0.0
    ).astype(BF16)
    wide = dot(tall, repeat)
    same = lax.div(iota((feat, feat), 0), levels) == lax.div(iota((feat, feat), 1), levels)
    return jnp.where(same, wide, 0.0)


def regroup(values):
    sub = iota(values.shape, 0)
    block = lax.div(iota(values.shape, 1), GROUP)
    for bit in (1, 2, 4):
        moved = pltpu.roll(values, LANES - GROUP * bit, 1)
        values = jnp.where((sub & bit) != 0, moved, values)
    for bit in (1, 2, 4):
        moved = pltpu.roll(values, bit, 0)
        values = jnp.where((block & bit) != 0, moved, values)
    return values


def build_stencil(nb_ref, cf_ref, code_ref, low_ref, coeff_ref, s_ref):
    points = nb_ref.shape[1]
    width = s_ref.shape[1]
    low_count = LANES
    high_count = width // low_count
    lane = iota((8, LANES), 1)
    for m in range(points // LANES):
        part = slice(m * LANES, (m + 1) * LANES)
        rows = slice(m * 8, (m + 1) * 8)
        index = regroup(nb_ref[:, part])
        code_ref[rows, :] = lax.div(index, low_count) * GROUP + (lane & (GROUP - 1))
        low_ref[rows, :] = index & (low_count - 1)
        coeff_ref[rows, :] = regroup(cf_ref[:, part])
    high_rows = iota((high_count * GROUP, LANES), 0)
    low_rows = iota((low_count, LANES), 0)
    unroll = 4

    def body(step, carry):
        for u in range(unroll):
            g = step * unroll + u
            high = jnp.where(high_rows == code_ref[pl.ds(g, 1), :], 1.0, 0.0).astype(BF16)
            low = jnp.where(low_rows == low_ref[pl.ds(g, 1), :], coeff_ref[pl.ds(g, 1), :], 0.0)
            out = dot(high, low.astype(BF16), 1, 1).astype(BF16)
            start = pl.multiple_of(g * GROUP, GROUP)
            for h in range(high_count):
                s_ref[pl.ds(start, GROUP), h * low_count : (h + 1) * low_count] = out[
                    h * GROUP : (h + 1) * GROUP
                ]
        return carry

    lax.fori_loop(0, points // GROUP // unroll, body, 0)


def one_hot_columns(row, height):
    return jnp.where(iota((height, LANES), 0) == row, 1.0, 0.0).astype(BF16)


def one_hot_of_rows(row, width):
    column = jnp.broadcast_to(row.astype(F32), (LANES, LANES)).T.astype(I32)
    lane = iota((LANES, LANES), 1)
    return jnp.concatenate(
        [
            jnp.where(column == lane + c * LANES, 1.0, 0.0).astype(BF16)
            for c in range(width // LANES)
        ],
        axis=1,
    )


def adjoint_kernel(
    live_ref, field_ref, send_ref, nb_ref, cf_ref, vert_ref, w_ref, map_ref, cot_ref,
    sent0, sent1, sent2, sent3, own_ref, s_ref, pt_ref,
    code_ref, low_ref, coeff_ref, bb_ref, mbt_ref, halo_ref,
):
    order = neighbor_order()
    points = field_ref.shape[0]
    half = send_ref.shape[1]
    slots, block = map_ref.shape
    live = live_ref[0, 0]
    for slot, sent in enumerate((sent0, sent1, sent2, sent3)):
        for h in range(half // LANES):
            cols = slice(h * LANES, (h + 1) * LANES)
            first = slot // 2 * 2
            row = jnp.where(
                order[slot] == first, send_ref[first : first + 1, cols], send_ref[first + 1 : first + 2, cols]
            )
            picked = dot(one_hot_of_rows(row, points), field_ref[...])
            sent[cols, :] = picked.astype(BF16)
    for j in range(slots):
        cols = slice(j * block, (j + 1) * block)
        pt_ref[:, cols] = one_hot_columns(map_ref[j : j + 1, :], points)
        result = dot(w_ref[j], cot_ref[cols, :], 0, 0)
        bb_ref[cols, :] = jnp.where(j < live, result, 0.0).astype(BF16)
    build_stencil(nb_ref, cf_ref, code_ref, low_ref, coeff_ref, s_ref)
    mixing = mixing_matrix(vert_ref).astype(BF16)
    rows_each = 256
    for c in range(points // rows_each):
        rows = slice(c * rows_each, (c + 1) * rows_each)
        back = dot(pt_ref[rows, :], bb_ref[...]).astype(BF16)
        mbt_ref[:, rows] = dot(mixing, back, 1, 1).astype(BF16)
    for c in range(s_ref.shape[1] // half):
        cols = slice(c * half, (c + 1) * half)
        part = dot(mbt_ref[...], s_ref[:, cols]).T
        if c * half < points:
            own_ref[cols, :] = part
        else:
            halo_ref[c * half - points : (c + 1) * half - points, :] = part.astype(BF16)
    for slot, sent in enumerate((sent0, sent1, sent2, sent3)):
        start = pl.multiple_of((order[slot] ^ 1) * half, half)
        sent[half:, :] = halo_ref[pl.ds(start, half), :]


def forward_kernel(
    live_ref, got0, got1, got2, got3, field_ref, send_ref, vert_ref, w_ref, own_ref, s_ref, pt_ref,
    grid_ref, grad_ref,
    ext_ref, ret_ref, conv_ref, sel_ref,
):
    order = neighbor_order()
    points = field_ref.shape[0]
    half = send_ref.shape[1]
    slots, block = w_ref.shape[0], w_ref.shape[1]
    live = live_ref[0, 0]
    ext_ref[:points, :] = field_ref[...]
    for slot, got in enumerate((got0, got1, got2, got3)):
        start = pl.multiple_of(points + (order[slot] ^ 1) * half, half)
        ext_ref[pl.ds(start, half), :] = got[:half, :]
        ret_ref[pl.ds(pl.multiple_of(order[slot] * half, half), half), :] = got[half:, :]
    mixing = mixing_matrix(vert_ref).T.astype(BF16)
    rows_each = 256
    for c in range(points // rows_each):
        rows = slice(c * rows_each, (c + 1) * rows_each)
        horizontal = dot(s_ref[rows, :], ext_ref[...]).astype(BF16)
        conv_ref[:, rows] = dot(mixing, horizontal, 1, 1).astype(BF16)
    for j in range(0, slots, 2):
        source = dot(conv_ref[...], pt_ref[:, j * block : (j + 2) * block]).astype(BF16)
        for u in range(2):
            result = dot(w_ref[j + u], source[:, u * block : (u + 1) * block], 1, 1)
            grid_ref[(j + u) * block : (j + u + 1) * block, :] = jnp.where(
                j + u < live, result, 0.0
            ).astype(BF16)
    for q in range(4):
        for h in range(half // LANES):
            cols = slice(q * half + h * LANES, q * half + (h + 1) * LANES)
            row = send_ref[q : q + 1, h * LANES : (h + 1) * LANES]
            sel_ref[:, cols] = one_hot_columns(row, points)
    for c in range(points // rows_each):
        rows = slice(c * rows_each, (c + 1) * rows_each)
        grad_ref[rows, :] = (own_ref[rows, :] + dot(sel_ref[rows, :], ret_ref[...])).astype(BF16)


def swap_pairs(count, first):
    pairs = [(i, (i + 1) % count) for i in range(first, count, 2)]
    return pairs + [(b, a) for a, b in pairs]


def exchange(value, axis, first, cycle):
    count = lax.axis_size(axis)
    pairs = swap_pairs(count, first)
    if not cycle:
        pairs = [(a, b) for a, b in pairs if abs(a - b) == 1]
    return lax.ppermute(value, axis, pairs)


def shards(field, grid_cotangent, send_rows, neighbors, stencil, vertical, interp_weights, block_map, tally):
    field = field[0, 0]
    cotangent = grid_cotangent[0, 0]
    send = send_rows[0, 0]
    nb = neighbors[0, 0].T
    cf = stencil[0, 0].T
    weights = interp_weights[0, 0]
    mapped = block_map[0, 0]
    vert = vertical.reshape(-1, vertical.shape[-1])
    points, feat = field.shape
    half = send.shape[1]
    width = points + 4 * half
    slots, block = mapped.shape
    vmem = pl.BlockSpec(memory_space=pltpu.VMEM)
    smem = pl.BlockSpec(memory_space=pltpu.SMEM)
    params = pltpu.CompilerParams(vmem_limit_bytes=VMEM_LIMIT)
    sent_shape = jax.ShapeDtypeStruct((2 * half, feat), BF16)
    sent0, sent1, sent2, sent3, own, s_mat, pt_mat = pl.pallas_call(
        adjoint_kernel,
        out_shape=(sent_shape,) * 4 + (
            jax.ShapeDtypeStruct((points, feat), F32),
            jax.ShapeDtypeStruct((points, width), BF16),
            jax.ShapeDtypeStruct((points, slots * block), BF16),
        ),
        in_specs=[smem] + [vmem] * 8,
        out_specs=(vmem,) * 7,
        scratch_shapes=[
            pltpu.VMEM((points // GROUP, LANES), I32),
            pltpu.VMEM((points // GROUP, LANES), I32),
            pltpu.VMEM((points // GROUP, LANES), F32),
            pltpu.VMEM((slots * block, feat), BF16),
            pltpu.VMEM((feat, points), BF16),
            pltpu.VMEM((4 * half, feat), BF16),
        ],
        compiler_params=params,
        cost_estimate=pl.CostEstimate(flops=10**9, bytes_accessed=8 * 10**6, transcendentals=0),
    )(tally, field, send, nb, cf, vert, weights, mapped, cotangent)
    got1 = exchange(sent1, "blk", 1, True)
    got3 = exchange(sent3, "tile", 1, False)
    got2 = exchange(sent2, "tile", 0, False)
    got0 = exchange(sent0, "blk", 0, True)
    grid, grad = pl.pallas_call(
        forward_kernel,
        out_shape=(
            jax.ShapeDtypeStruct((slots * block, feat), BF16),
            jax.ShapeDtypeStruct((points, feat), BF16),
        ),
        in_specs=[smem] + [vmem] * 11,
        out_specs=(vmem, vmem),
        scratch_shapes=[
            pltpu.VMEM((width, feat), BF16),
            pltpu.VMEM((4 * half, feat), BF16),
            pltpu.VMEM((feat, points), BF16),
            pltpu.VMEM((points, 4 * half), BF16),
        ],
        compiler_params=params,
        cost_estimate=pl.CostEstimate(flops=10**9, bytes_accessed=8 * 10**6, transcendentals=0),
    )(tally, got0, got1, got2, got3, field, send, vert, weights, own, s_mat, pt_mat)
    return grid[None, None], grad[None, None]


def solution(mesh):
    four = P("blk", "tile", None, None)
    in_specs = (four, four, four, four, four, P(), P("blk", "tile", None, None, None), four, P("blk", "tile"))
    return jax.shard_map(shards, mesh=mesh, in_specs=in_specs, out_specs=(four, four), check_vma=False)
```

```python
import jax
import jax.numpy as jnp
from jax import lax
from jax.experimental import pallas as pl
from jax.experimental.pallas import tpu as pltpu
from jax.sharding import PartitionSpec as P

MEMBERS = 4
LANES = 128
GROUP = 16
LOW = 256
CHUNK = 256
BF16 = jnp.bfloat16
F32 = jnp.float32
I32 = jnp.int32
VMEM_LIMIT = 20 * 1024 * 1024


def iota(shape, dim):
    return lax.broadcasted_iota(I32, shape, dim)


def dot(left, right, left_dim=1, right_dim=0):
    return lax.dot_general(
        left, right, (((left_dim,), (right_dim,)), ((), ())), preferred_element_type=F32
    )


def neighbor_order():
    blk_odd = lax.rem(lax.axis_index("blk"), 2)
    tile_odd = lax.rem(lax.axis_index("tile"), 2)
    return (blk_odd, 1 - blk_odd, 2 + tile_odd, 3 - tile_odd)


def mixing_matrix(vertical):
    levels = vertical.shape[1]
    tall = jnp.concatenate([vertical.astype(BF16)] * MEMBERS, axis=0)
    feat = tall.shape[0]
    repeat = jnp.where(
        lax.rem(iota((levels, feat), 1), levels) == iota((levels, feat), 0), 1.0, 0.0
    ).astype(BF16)
    wide = dot(tall, repeat)
    same = lax.div(iota((feat, feat), 0), levels) == lax.div(iota((feat, feat), 1), levels)
    return jnp.where(same, wide, 0.0)


def regroup(values):
    sub = iota(values.shape, 0)
    block = lax.div(iota(values.shape, 1), GROUP)
    for bit in (1, 2, 4):
        moved = pltpu.roll(values, LANES - GROUP * bit, 1)
        values = jnp.where((sub & bit) != 0, moved, values)
    for bit in (1, 2, 4):
        moved = pltpu.roll(values, bit, 0)
        values = jnp.where((block & bit) != 0, moved, values)
    return values


def build_stencil(nb_ref, cf_ref, code_ref, low_ref, coeff_ref, s_ref):
    points = nb_ref.shape[1]
    high_count = s_ref.shape[1] // LOW
    lane = iota((8, LANES), 1)
    for m in range(points // LANES):
        part = slice(m * LANES, (m + 1) * LANES)
        rows = slice(m * 8, (m + 1) * 8)
        index = regroup(nb_ref[:, part])
        code_ref[rows, :] = lax.div(index, LOW) * GROUP + (lane & (GROUP - 1))
        low_ref[rows, :] = index & (LOW - 1)
        coeff_ref[rows, :] = regroup(cf_ref[:, part])
    high_rows = iota((high_count * GROUP, LANES), 0)
    low_rows = iota((LOW, LANES), 0)
    for g in range(points // GROUP):
        high = jnp.where(high_rows == code_ref[g : g + 1, :], 1.0, 0.0).astype(BF16)
        low = jnp.where(low_rows == low_ref[g : g + 1, :], coeff_ref[g : g + 1, :], 0.0)
        out = dot(high, low.astype(BF16), 1, 1).astype(BF16)
        for h in range(high_count):
            s_ref[g * GROUP : (g + 1) * GROUP, h * LOW : (h + 1) * LOW] = out[
                h * GROUP : (h + 1) * GROUP
            ]


def one_hot_columns(row, height):
    return jnp.where(iota((height, LANES), 0) == row, 1.0, 0.0).astype(BF16)


def adjoint_kernel(
    live_ref, field_hbm, send_hbm, nb_hbm, cf_hbm, vert_hbm, w_hbm, map_hbm, cot_hbm,
    sent0, sent1, sent2, sent3, s_ref, pt_ref, mbt_ref, field_ref, send_ref, w_ref, mix_ref,
    nb_ref, cf_ref, vert_ref, map_ref, cot_ref,
    code_ref, low_ref, coeff_ref, bb_ref, back_ref, sems,
):
    order = neighbor_order()
    points = field_ref.shape[0]
    half = send_ref.shape[1]
    slots, block = map_ref.shape
    live = live_ref[0, 0]
    pairs = (
        (nb_hbm, nb_ref), (cf_hbm, cf_ref), (map_hbm, map_ref), (w_hbm, w_ref), (cot_hbm, cot_ref),
        (vert_hbm, vert_ref), (send_hbm, send_ref), (field_hbm, field_ref),
    )
    copies = [pltpu.make_async_copy(a, b, sems.at[i]) for i, (a, b) in enumerate(pairs)]
    for copy in copies:
        copy.start()
    copies[0].wait()
    copies[1].wait()
    build_stencil(nb_ref, cf_ref, code_ref, low_ref, coeff_ref, s_ref)
    for copy in copies[2:]:
        copy.wait()
    for j in range(slots):
        cols = slice(j * block, (j + 1) * block)
        pt_ref[:, cols] = one_hot_columns(map_ref[j : j + 1, :], points)
        result = dot(w_ref[j], cot_ref[cols, :], 0, 0)
        bb_ref[cols, :] = jnp.where(j < live, result, 0.0).astype(BF16)
    mixing = mixing_matrix(vert_ref[...])
    mix_ref[...] = mixing.T.astype(BF16)
    for c in range(points // CHUNK):
        rows = slice(c * CHUNK, (c + 1) * CHUNK)
        back_ref[rows, :] = dot(pt_ref[rows, :], bb_ref[...]).astype(BF16)
    mbt_ref[...] = dot(mixing.astype(BF16), back_ref[...], 1, 1).astype(BF16)
    field_t = field_ref[...].T
    for slot, sent in enumerate((sent0, sent1, sent2, sent3)):
        columns = []
        for h in range(half // LANES):
            lanes = slice(h * LANES, (h + 1) * LANES)
            first = slot // 2 * 2
            row = jnp.where(
                order[slot] == first, send_ref[first : first + 1, lanes], send_ref[first + 1 : first + 2, lanes]
            )
            columns.append(one_hot_columns(row, points))
        sent[:half, :] = dot(field_t, jnp.concatenate(columns, axis=1)).T.astype(BF16)
        start = pl.multiple_of(points + (order[slot] ^ 1) * half, half)
        sent[half:, :] = dot(mbt_ref[...], s_ref[:, pl.ds(start, half)]).T.astype(BF16)


def local_kernel(mbt_ref, s_ref, field_ref, send_ref, own_ref, hor_ref, sel_ref):
    points = field_ref.shape[0]
    half = send_ref.shape[1]
    for c in range(points // CHUNK):
        rows = slice(c * CHUNK, (c + 1) * CHUNK)
        own_ref[rows, :] = dot(mbt_ref[...], s_ref[:, rows]).T
        hor_ref[rows, :] = dot(s_ref[rows, :points], field_ref[...])
    for q in range(4):
        for h in range(half // LANES):
            cols = slice(q * half + h * LANES, q * half + (h + 1) * LANES)
            row = send_ref[q : q + 1, h * LANES : (h + 1) * LANES]
            sel_ref[:, cols] = one_hot_columns(row, points)


def forward_kernel(
    live_ref, got0, got1, got2, got3, s_ref, pt_ref, w_ref, mix_ref, own_ref, hor_ref, sel_ref,
    grid_hbm, grad_hbm,
    halo_ref, ret_ref, hb_ref, conv_ref, src_ref, grid_ref, grad_ref, sems,
):
    order = neighbor_order()
    points = hor_ref.shape[0]
    half = got0.shape[0] // 2
    slots, block = w_ref.shape[0], w_ref.shape[1]
    live = live_ref[0, 0]
    for slot, got in enumerate((got0, got1, got2, got3)):
        start = pl.multiple_of((order[slot] ^ 1) * half, half)
        halo_ref[pl.ds(start, half), :] = got[:half, :]
        ret_ref[pl.ds(pl.multiple_of(order[slot] * half, half), half), :] = got[half:, :]
    for c in range(points // CHUNK):
        rows = slice(c * CHUNK, (c + 1) * CHUNK)
        hb_ref[rows, :] = (hor_ref[rows, :] + dot(s_ref[rows, points:], halo_ref[...])).astype(BF16)
    conv_ref[...] = dot(mix_ref[...], hb_ref[...], 1, 1).astype(BF16)
    for c in range(points // CHUNK):
        rows = slice(c * CHUNK, (c + 1) * CHUNK)
        grad_ref[rows, :] = (own_ref[rows, :] + dot(sel_ref[rows, :], ret_ref[...])).astype(BF16)
    copies = [pltpu.make_async_copy(grad_ref, grad_hbm, sems.at[0])]
    copies[0].start()
    for c in range(slots * block // CHUNK):
        cols = slice(c * CHUNK, (c + 1) * CHUNK)
        src_ref[cols, :] = dot(conv_ref[...], pt_ref[:, cols]).T.astype(BF16)
    quarter = slots // 4
    for j in range(slots):
        rows = slice(j * block, (j + 1) * block)
        result = dot(w_ref[j], src_ref[rows, :])
        grid_ref[rows, :] = jnp.where(j < live, result, 0.0).astype(BF16)
        if j % quarter == quarter - 1:
            part = pl.ds((j + 1 - quarter) * block, quarter * block)
            copies.append(pltpu.make_async_copy(grid_ref.at[part], grid_hbm.at[part], sems.at[len(copies)]))
            copies[-1].start()
    for copy in copies:
        copy.wait()


def exchange(value, axis, first, cycle):
    count = lax.axis_size(axis)
    pairs = [(i, (i + 1) % count) for i in range(first, count, 2)]
    if not cycle:
        pairs = [(a, b) for a, b in pairs if a < b]
    return lax.ppermute(value, axis, pairs + [(b, a) for a, b in pairs])


def shards(field, grid_cotangent, send_rows, neighbors, stencil, vertical, interp_weights, block_map, tally):
    field = field[0, 0]
    cotangent = grid_cotangent[0, 0]
    send = send_rows[0, 0]
    nb = neighbors[0, 0].T
    cf = stencil[0, 0].T
    weights = interp_weights[0, 0]
    mapped = block_map[0, 0]
    vert = vertical.reshape(-1, vertical.shape[-1])
    points, feat = field.shape
    half = send.shape[1]
    width = points + 4 * half
    slots, block = mapped.shape
    vmem = pl.BlockSpec(memory_space=pltpu.VMEM)
    smem = pl.BlockSpec(memory_space=pltpu.SMEM)
    hbm = pl.BlockSpec(memory_space=pltpu.HBM)

    def in_vmem(*values):
        return [pltpu.with_memory_space_constraint(value, pltpu.VMEM) for value in values]

    def in_hbm(*values):
        return [pltpu.with_memory_space_constraint(value, pltpu.HBM) for value in values]

    def cost(flops):
        return pl.CostEstimate(flops=flops, bytes_accessed=10**6, transcendentals=0)

    params = pltpu.CompilerParams(vmem_limit_bytes=VMEM_LIMIT)
    shared = (
        pltpu.VMEM((points, width), BF16),
        pltpu.VMEM((points, slots * block), BF16),
        pltpu.VMEM((feat, points), BF16),
        pltpu.VMEM(field.shape, BF16),
        pltpu.VMEM(send.shape, I32),
        pltpu.VMEM(weights.shape, BF16),
        pltpu.VMEM((feat, feat), BF16),
    )
    sent0, sent1, sent2, sent3, s_mat, pt_mat, mbt, field_v, send_v, w_v, mix = pl.pallas_call(
        adjoint_kernel,
        out_shape=(pltpu.VMEM((2 * half, feat), BF16),) * 4 + shared,
        in_specs=[smem] + [hbm] * 8,
        out_specs=(vmem,) * 11,
        scratch_shapes=[
            pltpu.VMEM(nb.shape, I32),
            pltpu.VMEM(cf.shape, F32),
            pltpu.VMEM(vert.shape, F32),
            pltpu.VMEM(mapped.shape, I32),
            pltpu.VMEM(cotangent.shape, BF16),
            pltpu.VMEM((points // GROUP, LANES), I32),
            pltpu.VMEM((points // GROUP, LANES), I32),
            pltpu.VMEM((points // GROUP, LANES), F32),
            pltpu.VMEM((slots * block, feat), BF16),
            pltpu.VMEM((points, feat), BF16),
            pltpu.SemaphoreType.DMA((8,)),
        ],
        compiler_params=params,
        cost_estimate=cost(2 * 10**9),
    )(tally, *in_hbm(field, send, nb, cf, vert, weights, mapped, cotangent))
    got0 = exchange(sent0, "blk", 0, True)
    got1 = exchange(sent1, "blk", 1, True)
    got2 = exchange(sent2, "tile", 0, False)
    got3 = exchange(sent3, "tile", 1, False)
    own, hor, sel = pl.pallas_call(
        local_kernel,
        out_shape=(
            pltpu.VMEM((points, feat), F32),
            pltpu.VMEM((points, feat), F32),
            pltpu.VMEM((points, 4 * half), BF16),
        ),
        in_specs=[vmem] * 4,
        out_specs=(vmem,) * 3,
        compiler_params=params,
        cost_estimate=cost(10**9),
    )(*in_vmem(mbt, s_mat, field_v, send_v))
    grid, grad = pl.pallas_call(
        forward_kernel,
        out_shape=(
            pltpu.HBM((slots * block, feat), BF16),
            pltpu.HBM((points, feat), BF16),
        ),
        in_specs=[smem] + [vmem] * 11,
        out_specs=(hbm, hbm),
        scratch_shapes=[
            pltpu.VMEM((4 * half, feat), BF16),
            pltpu.VMEM((4 * half, feat), BF16),
            pltpu.VMEM((points, feat), BF16),
            pltpu.VMEM((feat, points), BF16),
            pltpu.VMEM((slots * block, feat), BF16),
            pltpu.VMEM((slots * block, feat), BF16),
            pltpu.VMEM((points, feat), BF16),
            pltpu.SemaphoreType.DMA((5,)),
        ],
        compiler_params=params,
        cost_estimate=cost(10**9),
    )(tally, *in_vmem(got0, got1, got2, got3, s_mat, pt_mat, w_v, mix, own, hor, sel))
    return grid[None, None], grad[None, None]


def solution(mesh):
    four = P("blk", "tile", None, None)
    in_specs = (four, four, four, four, four, P(), P("blk", "tile", None, None, None), four, P("blk", "tile"))
    return jax.shard_map(shards, mesh=mesh, in_specs=in_specs, out_specs=(four, four), check_vma=False)
```

```python
import jax
import jax.numpy as jnp
from jax import lax
from jax.experimental import pallas as pl
from jax.experimental.pallas import tpu as pltpu
from jax.sharding import PartitionSpec as P

MEMBERS = 4
LANES = 128
GROUP = 16
LOW = 256
CHUNK = 256
BF16 = jnp.bfloat16
F32 = jnp.float32
I32 = jnp.int32
SLOTS = (3, 2, 1, 0)
VMEM_LIMIT = 20 * 1024 * 1024


def iota(shape, dim):
    return lax.broadcasted_iota(I32, shape, dim)


def dot(left, right, left_dim=1, right_dim=0):
    return lax.dot_general(
        left, right, (((left_dim,), (right_dim,)), ((), ())), preferred_element_type=F32
    )


def neighbor_order():
    blk_odd = lax.rem(lax.axis_index("blk"), 2)
    tile_odd = lax.rem(lax.axis_index("tile"), 2)
    sent = (blk_odd, 1 - blk_odd, 2 + tile_odd, 3 - tile_odd)
    return [sent[kind] for kind in SLOTS]


def mixing_matrix(vertical):
    levels = vertical.shape[1]
    tall = jnp.concatenate([vertical.astype(BF16)] * MEMBERS, axis=0)
    feat = tall.shape[0]
    repeat = jnp.where(
        lax.rem(iota((levels, feat), 1), levels) == iota((levels, feat), 0), 1.0, 0.0
    ).astype(BF16)
    wide = dot(tall, repeat)
    same = lax.div(iota((feat, feat), 0), levels) == lax.div(iota((feat, feat), 1), levels)
    return jnp.where(same, wide, 0.0)


def regroup(values):
    sub = iota(values.shape, 0)
    block = lax.div(iota(values.shape, 1), GROUP)
    for bit in (1, 2, 4):
        moved = pltpu.roll(values, LANES - GROUP * bit, 1)
        values = jnp.where((sub & bit) != 0, moved, values)
    for bit in (1, 2, 4):
        moved = pltpu.roll(values, bit, 0)
        values = jnp.where((block & bit) != 0, moved, values)
    return values


def build_stencil(nb_ref, cf_ref, code_ref, low_ref, coeff_ref, s_ref):
    points = nb_ref.shape[1]
    high_count = s_ref.shape[1] // LOW
    lane = iota((8, LANES), 1)
    for m in range(points // LANES):
        part = slice(m * LANES, (m + 1) * LANES)
        rows = slice(m * 8, (m + 1) * 8)
        index = regroup(nb_ref[:, part])
        code_ref[rows, :] = (lax.div(index, LOW) * GROUP + (lane & (GROUP - 1))).astype(F32)
        low_ref[rows, :] = (index & (LOW - 1)).astype(F32)
        coeff_ref[rows, :] = regroup(cf_ref[:, part])
    high_rows = iota((high_count * GROUP, LANES), 0).astype(F32).astype(BF16)
    low_rows = iota((LOW, LANES), 0).astype(F32).astype(BF16)
    one, zero = jnp.ones((), BF16), jnp.zeros((), BF16)
    for g in range(points // GROUP):
        code, low_row, coeff = (ref[g : g + 1, :].astype(BF16) for ref in (code_ref, low_ref, coeff_ref))
        high = jnp.where(high_rows == code, one, zero)
        low = jnp.where(low_rows == low_row, coeff, zero)
        out = dot(high, low, 1, 1).astype(BF16)
        for h in range(high_count):
            s_ref[g * GROUP : (g + 1) * GROUP, h * LOW : (h + 1) * LOW] = out[
                h * GROUP : (h + 1) * GROUP
            ]


def one_hot_columns(row, height):
    return jnp.where(iota((height, LANES), 0) == row, 1.0, 0.0).astype(BF16)


def one_hot_rows(row, width):
    column = jnp.broadcast_to(row.astype(F32), (LANES, LANES)).T
    lane = iota((LANES, LANES), 1).astype(F32)
    parts = [jnp.where(column == lane + float(c * LANES), 1.0, 0.0) for c in range(width // LANES)]
    return jnp.concatenate([part.astype(BF16) for part in parts], axis=1)


def send_selector(send_ref, slot, direction, points):
    half = send_ref.shape[1]
    first = SLOTS[slot] // 2 * 2
    columns = []
    for h in range(half // LANES):
        lanes = slice(h * LANES, (h + 1) * LANES)
        row = jnp.where(
            direction == first, send_ref[first : first + 1, lanes], send_ref[first + 1 : first + 2, lanes]
        )
        columns.append(one_hot_columns(row, points))
    return jnp.concatenate(columns, axis=1)


def halo_part(ref, rows, direction, points, half):
    return ref[rows, pl.ds(pl.multiple_of(points + (direction ^ 1) * half, half), half)]


def adjoint_kernel(
    live_ref, field_hbm, send_hbm, nb_hbm, cf_hbm, vert_hbm, w_hbm, map_hbm, cot_hbm,
    sent0, sent1, sent2, sent3, s_ref, mbt_ref, field_ref, send_ref, w_ref, mix_ref, map_ref,
    nb_ref, cf_ref, vert_ref, cot_ref,
    code_ref, low_ref, coeff_ref, p_ref, bbt_ref, back_ref, sems,
):
    order = neighbor_order()
    points = field_ref.shape[0]
    half = send_ref.shape[1]
    slots, block = map_ref.shape
    live = live_ref[0, 0]
    pairs = (
        (nb_hbm, nb_ref), (cf_hbm, cf_ref), (map_hbm, map_ref), (w_hbm, w_ref), (cot_hbm, cot_ref),
        (vert_hbm, vert_ref), (send_hbm, send_ref), (field_hbm, field_ref),
    )
    copies = [pltpu.make_async_copy(a, b, sems.at[i]) for i, (a, b) in enumerate(pairs)]
    for copy in copies:
        copy.start()
    copies[0].wait()
    copies[1].wait()
    build_stencil(nb_ref, cf_ref, code_ref, low_ref, coeff_ref, s_ref)
    for copy in copies[2:]:
        copy.wait()
    for j in range(slots):
        rows = slice(j * block, (j + 1) * block)
        p_ref[rows, :] = one_hot_rows(map_ref[j : j + 1, :], points)
        result = dot(cot_ref[rows, :], w_ref[j], 0, 0)
        bbt_ref[:, rows] = jnp.where(j < live, result, 0.0).astype(BF16)
    mixing = mixing_matrix(vert_ref[...])
    mix_ref[...] = mixing.T.astype(BF16)
    for c in range(points // CHUNK):
        cols = slice(c * CHUNK, (c + 1) * CHUNK)
        back_ref[:, cols] = dot(bbt_ref[...], p_ref[:, cols]).astype(BF16)
    mbt_ref[...] = dot(mixing.astype(BF16), back_ref[...]).astype(BF16)
    field_t = field_ref[...].T
    for slot, sent in enumerate((sent0, sent1, sent2, sent3)):
        sent[:half, :] = dot(field_t, send_selector(send_ref, slot, order[slot], points)).T.astype(BF16)
        part = halo_part(s_ref, slice(None), order[slot], points, half)
        sent[half:, :] = dot(mbt_ref[...], part).T.astype(BF16)


def local_kernel(
    got0, got1, mbt_ref, s_ref, field_ref, send_ref, map_ref, own_ref, hor_ref, sel_ref, pt_ref, tile_ref
):
    order = neighbor_order()
    points = field_ref.shape[0]
    half = send_ref.shape[1]
    slots, block = map_ref.shape
    for slot in range(4):
        target = tile_ref if slot < 2 else sel_ref
        start = slot % 2 * half
        target[:, start : start + half] = send_selector(send_ref, slot, order[slot], points)
    for j in range(slots):
        pt_ref[:, j * block : (j + 1) * block] = one_hot_columns(map_ref[j : j + 1, :], points)
    for c in range(points // CHUNK):
        rows = slice(c * CHUNK, (c + 1) * CHUNK)
        own = dot(mbt_ref[...], s_ref[:, rows]).T
        own = own + dot(tile_ref[rows, :half], got0[half:, :])
        own_ref[rows, :] = own + dot(tile_ref[rows, half:], got1[half:, :])
        hor = dot(s_ref[rows, :points], field_ref[...])
        hor = hor + dot(halo_part(s_ref, rows, order[0], points, half), got0[:half, :])
        hor_ref[rows, :] = hor + dot(halo_part(s_ref, rows, order[1], points, half), got1[:half, :])


def forward_kernel(
    live_ref, got2, got3, s_ref, pt_ref, w_ref, mix_ref, own_ref, hor_ref, sel_ref,
    grid_hbm, grad_hbm,
    hb_ref, conv_ref, src_ref, grid_ref, grad_ref, sems,
):
    order = neighbor_order()
    points = hor_ref.shape[0]
    half = got2.shape[0] // 2
    slots, block = w_ref.shape[0], w_ref.shape[1]
    live = live_ref[0, 0]
    for c in range(points // CHUNK):
        rows = slice(c * CHUNK, (c + 1) * CHUNK)
        hor = hor_ref[rows, :] + dot(halo_part(s_ref, rows, order[2], points, half), got2[:half, :])
        hor = hor + dot(halo_part(s_ref, rows, order[3], points, half), got3[:half, :])
        hb_ref[rows, :] = hor.astype(BF16)
    conv_ref[...] = dot(mix_ref[...], hb_ref[...], 1, 1).astype(BF16)
    for c in range(points // CHUNK):
        rows = slice(c * CHUNK, (c + 1) * CHUNK)
        own = own_ref[rows, :] + dot(sel_ref[rows, :half], got2[half:, :])
        grad_ref[rows, :] = (own + dot(sel_ref[rows, half:], got3[half:, :])).astype(BF16)
    copies = [pltpu.make_async_copy(grad_ref, grad_hbm, sems.at[0])]
    copies[0].start()
    for c in range(slots * block // CHUNK):
        cols = slice(c * CHUNK, (c + 1) * CHUNK)
        src_ref[cols, :] = dot(conv_ref[...], pt_ref[:, cols]).T.astype(BF16)
    quarter = slots // 4
    for j in range(slots):
        rows = slice(j * block, (j + 1) * block)
        result = dot(w_ref[j], src_ref[rows, :])
        grid_ref[rows, :] = jnp.where(j < live, result, 0.0).astype(BF16)
        if j % quarter == quarter - 1:
            part = pl.ds((j + 1 - quarter) * block, quarter * block)
            copies.append(pltpu.make_async_copy(grid_ref.at[part], grid_hbm.at[part], sems.at[len(copies)]))
            copies[-1].start()
    for copy in copies:
        copy.wait()


def exchange(value, axis, first, cycle):
    count = lax.axis_size(axis)
    pairs = [(i, (i + 1) % count) for i in range(first, count, 2)]
    if not cycle:
        pairs = [(a, b) for a, b in pairs if a < b]
    return lax.ppermute(value, axis, pairs + [(b, a) for a, b in pairs])


def shards(field, grid_cotangent, send_rows, neighbors, stencil, vertical, interp_weights, block_map, tally):
    field = field[0, 0]
    cotangent = grid_cotangent[0, 0]
    send = send_rows[0, 0]
    nb = neighbors[0, 0].T
    cf = stencil[0, 0].T
    weights = interp_weights[0, 0]
    mapped = block_map[0, 0]
    vert = vertical.reshape(-1, vertical.shape[-1])
    points, feat = field.shape
    half = send.shape[1]
    width = points + 4 * half
    slots, block = mapped.shape
    vmem = pl.BlockSpec(memory_space=pltpu.VMEM)
    smem = pl.BlockSpec(memory_space=pltpu.SMEM)
    hbm = pl.BlockSpec(memory_space=pltpu.HBM)

    def in_vmem(*values):
        return [pltpu.with_memory_space_constraint(value, pltpu.VMEM) for value in values]

    def in_hbm(*values):
        return [pltpu.with_memory_space_constraint(value, pltpu.HBM) for value in values]

    def cost(flops):
        return pl.CostEstimate(flops=flops, bytes_accessed=10**6, transcendentals=0)

    params = pltpu.CompilerParams(vmem_limit_bytes=VMEM_LIMIT)
    shared = (
        pltpu.VMEM((points, width), BF16),
        pltpu.VMEM((feat, points), BF16),
        pltpu.VMEM(field.shape, BF16),
        pltpu.VMEM(send.shape, I32),
        pltpu.VMEM(weights.shape, BF16),
        pltpu.VMEM((feat, feat), BF16),
        pltpu.VMEM(mapped.shape, I32),
    )
    sent0, sent1, sent2, sent3, s_mat, mbt, field_v, send_v, w_v, mix, map_v = pl.pallas_call(
        adjoint_kernel,
        out_shape=(pltpu.VMEM((2 * half, feat), BF16),) * 4 + shared,
        in_specs=[smem] + [hbm] * 8,
        out_specs=(vmem,) * 11,
        scratch_shapes=[
            pltpu.VMEM(nb.shape, I32),
            pltpu.VMEM(cf.shape, F32),
            pltpu.VMEM(vert.shape, F32),
            pltpu.VMEM(cotangent.shape, BF16),
            pltpu.VMEM((points // GROUP, LANES), F32),
            pltpu.VMEM((points // GROUP, LANES), F32),
            pltpu.VMEM((points // GROUP, LANES), F32),
            pltpu.VMEM((slots * block, points), BF16),
            pltpu.VMEM((feat, slots * block), BF16),
            pltpu.VMEM((feat, points), BF16),
            pltpu.SemaphoreType.DMA((8,)),
        ],
        compiler_params=params,
        cost_estimate=cost(2 * 10**9),
    )(tally, *in_hbm(field, send, nb, cf, vert, weights, mapped, cotangent))
    got0, got1, got2, got3 = (
        exchange(sent, ("blk", "tile")[kind // 2], kind % 2, kind < 2)
        for kind, sent in zip(SLOTS, (sent0, sent1, sent2, sent3))
    )
    own, hor, sel, pt_mat = pl.pallas_call(
        local_kernel,
        out_shape=(
            pltpu.VMEM((points, feat), F32),
            pltpu.VMEM((points, feat), F32),
            pltpu.VMEM((points, 2 * half), BF16),
            pltpu.VMEM((points, slots * block), BF16),
        ),
        in_specs=[vmem] * 7,
        out_specs=(vmem,) * 4,
        scratch_shapes=[pltpu.VMEM((points, 2 * half), BF16)],
        compiler_params=params,
        cost_estimate=cost(10**9),
    )(*in_vmem(got0, got1, mbt, s_mat, field_v, send_v, map_v))
    grid, grad = pl.pallas_call(
        forward_kernel,
        out_shape=(
            pltpu.HBM((slots * block, feat), BF16),
            pltpu.HBM((points, feat), BF16),
        ),
        in_specs=[smem] + [vmem] * 9,
        out_specs=(hbm, hbm),
        scratch_shapes=[
            pltpu.VMEM((points, feat), BF16),
            pltpu.VMEM((feat, points), BF16),
            pltpu.VMEM((slots * block, feat), BF16),
            pltpu.VMEM((slots * block, feat), BF16),
            pltpu.VMEM((points, feat), BF16),
            pltpu.SemaphoreType.DMA((5,)),
        ],
        compiler_params=params,
        cost_estimate=cost(10**9),
    )(tally, *in_vmem(got2, got3, s_mat, pt_mat, w_v, mix, own, hor, sel))
    return grid[None, None], grad[None, None]


def solution(mesh):
    four = P("blk", "tile", None, None)
    in_specs = (four, four, four, four, four, P(), P("blk", "tile", None, None, None), four, P("blk", "tile"))
    return jax.shard_map(shards, mesh=mesh, in_specs=in_specs, out_specs=(four, four), check_vma=False)
```

```python
import jax
import jax.numpy as jnp
from jax import lax
from jax.experimental import pallas as pl
from jax.experimental.pallas import tpu as pltpu
from jax.sharding import PartitionSpec as P

MEMBERS = 4
LANES = 128
GROUP = 16
LOW = 256
CHUNK = 256
BF16 = jnp.bfloat16
F32 = jnp.float32
I32 = jnp.int32
SLOTS = (3, 2, 1, 0)
ROW = 8
VMEM_LIMIT = 20 * 1024 * 1024


def iota(shape, dim):
    return lax.broadcasted_iota(I32, shape, dim)


def dot(left, right, left_dim=1, right_dim=0):
    return lax.dot_general(
        left, right, (((left_dim,), (right_dim,)), ((), ())), preferred_element_type=F32
    )


def neighbor_order():
    blk_odd = lax.rem(lax.axis_index("blk"), 2)
    tile_odd = lax.rem(lax.axis_index("tile"), 2)
    sent = (blk_odd, 1 - blk_odd, 2 + tile_odd, 3 - tile_odd)
    return [sent[kind] for kind in SLOTS]


def mixing_matrix(vertical):
    levels = vertical.shape[1]
    tall = jnp.concatenate([vertical.astype(BF16)] * MEMBERS, axis=0)
    feat = tall.shape[0]
    repeat = jnp.where(
        lax.rem(iota((levels, feat), 1), levels) == iota((levels, feat), 0), 1.0, 0.0
    ).astype(BF16)
    wide = dot(tall, repeat)
    same = lax.div(iota((feat, feat), 0), levels) == lax.div(iota((feat, feat), 1), levels)
    return jnp.where(same, wide, 0.0)


def regroup(values):
    sub = iota(values.shape, 0)
    block = lax.div(iota(values.shape, 1), GROUP)
    for bit in (1, 2, 4):
        moved = pltpu.roll(values, LANES - GROUP * bit, 1)
        values = jnp.where((sub & bit) != 0, moved, values)
    for bit in (1, 2, 4):
        moved = pltpu.roll(values, bit, 0)
        values = jnp.where((block & bit) != 0, moved, values)
    return values


def build_stencil(nb_ref, cf_ref, code_ref, low_ref, coeff_ref, s_ref):
    points = nb_ref.shape[1]
    high_count = s_ref.shape[1] // LOW
    lane = iota((8, LANES), 1)
    for m in range(points // LANES):
        part = slice(m * LANES, (m + 1) * LANES)
        rows = slice(m * 8, (m + 1) * 8)
        index = regroup(nb_ref[:, part])
        code_ref[rows, :] = (lax.div(index, LOW) * GROUP + (lane & (GROUP - 1))).astype(F32)
        low_ref[rows, :] = (index & (LOW - 1)).astype(F32)
        coeff_ref[rows, :] = regroup(cf_ref[:, part])
    high_rows = iota((high_count * GROUP, LANES), 0).astype(F32).astype(BF16)
    low_rows = iota((LOW, LANES), 0).astype(F32).astype(BF16)
    one, zero = jnp.ones((), BF16), jnp.zeros((), BF16)
    for g in range(points // GROUP):
        code, low_row, coeff = (ref[g : g + 1, :].astype(BF16) for ref in (code_ref, low_ref, coeff_ref))
        high = jnp.where(high_rows == code, one, zero)
        low = jnp.where(low_rows == low_row, coeff, zero)
        out = dot(high, low, 1, 1).astype(BF16)
        for h in range(high_count):
            s_ref[g * GROUP : (g + 1) * GROUP, h * LOW : (h + 1) * LOW] = out[
                h * GROUP : (h + 1) * GROUP
            ]


def one_hot_columns(row, height):
    return jnp.where(iota((height, LANES), 0) == row, 1.0, 0.0).astype(BF16)


def one_hot_rows(row, width):
    column = jnp.broadcast_to(row.astype(F32), (LANES, LANES)).T
    lane = iota((LANES, LANES), 1).astype(F32)
    parts = [jnp.where(column == lane + float(c * LANES), 1.0, 0.0) for c in range(width // LANES)]
    return jnp.concatenate([part.astype(BF16) for part in parts], axis=1)


def send_selector(send_ref, slot, direction, points):
    half = send_ref.shape[1]
    first = SLOTS[slot] // 2 * 2
    columns = []
    for h in range(half // LANES):
        lanes = slice(h * LANES, (h + 1) * LANES)
        row = jnp.where(
            direction == first, send_ref[first : first + 1, lanes], send_ref[first + 1 : first + 2, lanes]
        )
        columns.append(one_hot_columns(row, points))
    return jnp.concatenate(columns, axis=1)


def halo_part(ref, rows, direction, points, half):
    return ref[rows, pl.ds(pl.multiple_of(points + (direction ^ 1) * half, half), half)]


def adjoint_kernel(
    live_ref, field_hbm, send_hbm, nb_hbm, cf_hbm, vert_hbm, w_hbm, map_hbm, cot_hbm,
    sent0, sent1, sent2, sent3, s_ref, mbt_ref, field_ref, send_ref, w_ref, mix_ref, map_ref,
    nb_ref, cf_ref, vert_ref, cot_ref,
    code_ref, low_ref, coeff_ref, p_ref, bbt_ref, back_ref, sems,
):
    order = neighbor_order()
    points = field_ref.shape[0]
    half = send_ref.shape[1]
    slots, block = map_ref.shape
    live = live_ref[0, 0]
    pairs = (
        (nb_hbm, nb_ref), (cf_hbm, cf_ref), (map_hbm, map_ref), (w_hbm, w_ref), (cot_hbm, cot_ref),
        (vert_hbm, vert_ref), (send_hbm, send_ref), (field_hbm, field_ref),
    )
    copies = [pltpu.make_async_copy(a, b, sems.at[i]) for i, (a, b) in enumerate(pairs)]
    for copy in copies:
        copy.start()
    copies[0].wait()
    copies[1].wait()
    build_stencil(nb_ref, cf_ref, code_ref, low_ref, coeff_ref, s_ref)
    for copy in copies[2:]:
        copy.wait()
    for j in range(slots):
        rows = slice(j * block, (j + 1) * block)
        p_ref[rows, :] = one_hot_rows(map_ref[j : j + 1, :], points)
        result = dot(cot_ref[rows, :], w_ref[j], 0, 0)
        bbt_ref[:, rows] = jnp.where(j < live, result, 0.0).astype(BF16)
    mixing = mixing_matrix(vert_ref[...])
    mix_ref[...] = mixing.T.astype(BF16)
    for c in range(points // CHUNK):
        cols = slice(c * CHUNK, (c + 1) * CHUNK)
        back_ref[:, cols] = dot(bbt_ref[...], p_ref[:, cols]).astype(BF16)
    mbt_ref[...] = dot(mixing.astype(BF16), back_ref[...]).astype(BF16)
    field_t = field_ref[...].T
    for slot, sent in enumerate((sent0, sent1, sent2, sent3)):
        sent[:half, :] = dot(field_t, send_selector(send_ref, slot, order[slot], points)).T.astype(BF16)
        part = halo_part(s_ref, slice(None), order[slot], points, half)
        sent[half:, :] = dot(mbt_ref[...], part).T.astype(BF16)


def far_neighbor():
    place = lax.rem(lax.axis_index("blk"), ROW)
    return jnp.logical_or(place == 0, place == ROW - 1)


def early_kernel(*refs):
    pl.when(jnp.logical_not(far_neighbor()))(lambda: local_work(*refs[:7], *refs[8:12], refs[13]))


def late_kernel(*refs):
    pl.when(far_neighbor())(lambda: local_work(*refs[:7], *refs[11:]))


def local_work(
    got0, got1, mbt_ref, s_ref, field_ref, send_ref, map_ref, own_ref, hor_ref, sel_ref, pt_ref, tile_ref
):
    order = neighbor_order()
    points = field_ref.shape[0]
    half = send_ref.shape[1]
    slots, block = map_ref.shape
    for slot in range(4):
        target = tile_ref if slot < 2 else sel_ref
        start = slot % 2 * half
        target[:, start : start + half] = send_selector(send_ref, slot, order[slot], points)
    index = map_ref[...]
    low = (index & (LANES - 1)).astype(F32).astype(BF16)
    high = lax.div(index, LANES)
    row_ids = iota((LANES, LANES), 0).astype(F32).astype(BF16)
    for p in range(points // LANES):
        here = jnp.where(high == p, 1.0, 0.0).astype(BF16)
        for j in range(slots):
            pt_ref[p * LANES : (p + 1) * LANES, j * block : (j + 1) * block] = jnp.where(
                row_ids == low[j : j + 1], here[j : j + 1], jnp.zeros((), BF16)
            )
    for c in range(points // CHUNK):
        rows = slice(c * CHUNK, (c + 1) * CHUNK)
        own = dot(mbt_ref[...], s_ref[:, rows]).T
        own = own + dot(tile_ref[rows, :half], got0[half:, :])
        own_ref[rows, :] = own + dot(tile_ref[rows, half:], got1[half:, :])
        hor = dot(s_ref[rows, :points], field_ref[...])
        hor = hor + dot(halo_part(s_ref, rows, order[0], points, half), got0[:half, :])
        hor_ref[rows, :] = hor + dot(halo_part(s_ref, rows, order[1], points, half), got1[:half, :])


def forward_kernel(
    live_ref, got2, got3, s_ref, pt_ref, w_ref, mix_ref, own_ref, hor_ref, sel_ref,
    grid_hbm, grad_hbm,
    hb_ref, conv_ref, src_ref, grid_ref, grad_ref, sems,
):
    order = neighbor_order()
    points = hor_ref.shape[0]
    half = got2.shape[0] // 2
    slots, block = w_ref.shape[0], w_ref.shape[1]
    live = live_ref[0, 0]
    for c in range(points // CHUNK):
        rows = slice(c * CHUNK, (c + 1) * CHUNK)
        hor = hor_ref[rows, :] + dot(halo_part(s_ref, rows, order[2], points, half), got2[:half, :])
        hor = hor + dot(halo_part(s_ref, rows, order[3], points, half), got3[:half, :])
        hb_ref[rows, :] = hor.astype(BF16)
    conv_ref[...] = dot(mix_ref[...], hb_ref[...], 1, 1).astype(BF16)
    for c in range(points // CHUNK):
        rows = slice(c * CHUNK, (c + 1) * CHUNK)
        own = own_ref[rows, :] + dot(sel_ref[rows, :half], got2[half:, :])
        grad_ref[rows, :] = (own + dot(sel_ref[rows, half:], got3[half:, :])).astype(BF16)
    copies = [pltpu.make_async_copy(grad_ref, grad_hbm, sems.at[0])]
    copies[0].start()
    for c in range(slots * block // CHUNK):
        cols = slice(c * CHUNK, (c + 1) * CHUNK)
        src_ref[cols, :] = dot(conv_ref[...], pt_ref[:, cols]).T.astype(BF16)
    quarter = slots // 4
    for j in range(slots):
        rows = slice(j * block, (j + 1) * block)
        result = dot(w_ref[j], src_ref[rows, :])
        grid_ref[rows, :] = jnp.where(j < live, result, 0.0).astype(BF16)
        if j % quarter == quarter - 1:
            part = pl.ds((j + 1 - quarter) * block, quarter * block)
            copies.append(pltpu.make_async_copy(grid_ref.at[part], grid_hbm.at[part], sems.at[len(copies)]))
            copies[-1].start()
    for copy in copies:
        copy.wait()


def exchange(value, axis, first, cycle):
    count = lax.axis_size(axis)
    pairs = [(i, (i + 1) % count) for i in range(first, count, 2)]
    if not cycle:
        pairs = [(a, b) for a, b in pairs if a < b]
    return lax.ppermute(value, axis, pairs + [(b, a) for a, b in pairs])


def shards(field, grid_cotangent, send_rows, neighbors, stencil, vertical, interp_weights, block_map, tally):
    field = field[0, 0]
    cotangent = grid_cotangent[0, 0]
    send = send_rows[0, 0]
    nb = neighbors[0, 0].T
    cf = stencil[0, 0].T
    weights = interp_weights[0, 0]
    mapped = block_map[0, 0]
    vert = vertical.reshape(-1, vertical.shape[-1])
    points, feat = field.shape
    half = send.shape[1]
    width = points + 4 * half
    slots, block = mapped.shape
    vmem = pl.BlockSpec(memory_space=pltpu.VMEM)
    smem = pl.BlockSpec(memory_space=pltpu.SMEM)
    hbm = pl.BlockSpec(memory_space=pltpu.HBM)

    def in_vmem(*values):
        return [pltpu.with_memory_space_constraint(value, pltpu.VMEM) for value in values]

    def in_hbm(*values):
        return [pltpu.with_memory_space_constraint(value, pltpu.HBM) for value in values]

    def cost(flops):
        return pl.CostEstimate(flops=flops, bytes_accessed=10**6, transcendentals=0)

    params = pltpu.CompilerParams(vmem_limit_bytes=VMEM_LIMIT)
    shared = (
        pltpu.VMEM((points, width), BF16),
        pltpu.VMEM((feat, points), BF16),
        pltpu.VMEM(field.shape, BF16),
        pltpu.VMEM(send.shape, I32),
        pltpu.VMEM(weights.shape, BF16),
        pltpu.VMEM((feat, feat), BF16),
        pltpu.VMEM(mapped.shape, I32),
    )
    sent0, sent1, sent2, sent3, s_mat, mbt, field_v, send_v, w_v, mix, map_v = pl.pallas_call(
        adjoint_kernel,
        out_shape=(pltpu.VMEM((2 * half, feat), BF16),) * 4 + shared,
        in_specs=[smem] + [hbm] * 8,
        out_specs=(vmem,) * 11,
        scratch_shapes=[
            pltpu.VMEM(nb.shape, I32),
            pltpu.VMEM(cf.shape, F32),
            pltpu.VMEM(vert.shape, F32),
            pltpu.VMEM(cotangent.shape, BF16),
            pltpu.VMEM((points // GROUP, LANES), F32),
            pltpu.VMEM((points // GROUP, LANES), F32),
            pltpu.VMEM((points // GROUP, LANES), F32),
            pltpu.VMEM((slots * block, points), BF16),
            pltpu.VMEM((feat, slots * block), BF16),
            pltpu.VMEM((feat, points), BF16),
            pltpu.SemaphoreType.DMA((8,)),
        ],
        compiler_params=params,
        cost_estimate=cost(2 * 10**9),
    )(tally, *in_hbm(field, send, nb, cf, vert, weights, mapped, cotangent))
    def trade(slot, sent):
        kind = SLOTS[slot]
        return exchange(sent, ("blk", "tile")[kind // 2], kind % 2, kind < 2)

    got0, got1, got2 = trade(0, sent0), trade(1, sent1), trade(2, sent2)
    local_shapes = (
        pltpu.VMEM((points, feat), F32),
        pltpu.VMEM((points, feat), F32),
        pltpu.VMEM((points, 2 * half), BF16),
        pltpu.VMEM((points, slots * block), BF16),
    )
    shared = (got0, got1, mbt, s_mat, field_v, send_v, map_v)
    *local, sent3 = pl.pallas_call(
        early_kernel,
        out_shape=local_shapes + (pltpu.VMEM(sent3.shape, BF16),),
        in_specs=[vmem] * 8,
        out_specs=(vmem,) * 5,
        scratch_shapes=[pltpu.VMEM((points, 2 * half), BF16)],
        input_output_aliases={7: 4},
        compiler_params=params,
        cost_estimate=cost(10**9),
    )(*in_vmem(*shared, sent3))
    got3 = trade(3, sent3)
    own, hor, sel, pt_mat = pl.pallas_call(
        late_kernel,
        out_shape=local_shapes,
        in_specs=[vmem] * 11,
        out_specs=(vmem,) * 4,
        scratch_shapes=[pltpu.VMEM((points, 2 * half), BF16)],
        input_output_aliases={7 + i: i for i in range(4)},
        compiler_params=params,
        cost_estimate=cost(10**9),
    )(*in_vmem(*shared, *local))
    grid, grad = pl.pallas_call(
        forward_kernel,
        out_shape=(
            pltpu.HBM((slots * block, feat), BF16),
            pltpu.HBM((points, feat), BF16),
        ),
        in_specs=[smem] + [vmem] * 9,
        out_specs=(hbm, hbm),
        scratch_shapes=[
            pltpu.VMEM((points, feat), BF16),
            pltpu.VMEM((feat, points), BF16),
            pltpu.VMEM((slots * block, feat), BF16),
            pltpu.VMEM((slots * block, feat), BF16),
            pltpu.VMEM((points, feat), BF16),
            pltpu.SemaphoreType.DMA((5,)),
        ],
        compiler_params=params,
        cost_estimate=cost(10**9),
    )(tally, *in_vmem(got2, got3, s_mat, pt_mat, w_v, mix, own, hor, sel))
    return grid[None, None], grad[None, None]


def solution(mesh):
    four = P("blk", "tile", None, None)
    in_specs = (four, four, four, four, four, P(), P("blk", "tile", None, None, None), four, P("blk", "tile"))
    return jax.shard_map(shards, mesh=mesh, in_specs=in_specs, out_specs=(four, four), check_vma=False)
```

```python
import jax
import jax.numpy as jnp
from jax import lax
from jax.experimental import pallas as pl
from jax.experimental.pallas import tpu as pltpu
from jax.sharding import PartitionSpec as P

MEMBERS = 4
LANES = 128
GROUP = 16
LOW = 256
CHUNK = 256
BF16 = jnp.bfloat16
F32 = jnp.float32
I32 = jnp.int32
SLOTS = (3, 2, 1, 0)
VMEM_LIMIT = 20 * 1024 * 1024


def iota(shape, dim):
    return lax.broadcasted_iota(I32, shape, dim)


def dot(left, right, left_dim=1, right_dim=0):
    return lax.dot_general(
        left, right, (((left_dim,), (right_dim,)), ((), ())), preferred_element_type=F32
    )


def neighbor_order():
    blk_odd = lax.rem(lax.axis_index("blk"), 2)
    tile_odd = lax.rem(lax.axis_index("tile"), 2)
    sent = (blk_odd, 1 - blk_odd, 2 + tile_odd, 3 - tile_odd)
    return [sent[kind] for kind in SLOTS]


def mixing_matrix(vertical):
    levels = vertical.shape[1]
    tall = jnp.concatenate([vertical.astype(BF16)] * MEMBERS, axis=0)
    feat = tall.shape[0]
    repeat = jnp.where(
        lax.rem(iota((levels, feat), 1), levels) == iota((levels, feat), 0), 1.0, 0.0
    ).astype(BF16)
    wide = dot(tall, repeat)
    same = lax.div(iota((feat, feat), 0), levels) == lax.div(iota((feat, feat), 1), levels)
    return jnp.where(same, wide, 0.0)


def regroup(values):
    sub = iota(values.shape, 0)
    block = lax.div(iota(values.shape, 1), GROUP)
    for bit in (1, 2, 4):
        moved = pltpu.roll(values, LANES - GROUP * bit, 1)
        values = jnp.where((sub & bit) != 0, moved, values)
    for bit in (1, 2, 4):
        moved = pltpu.roll(values, bit, 0)
        values = jnp.where((block & bit) != 0, moved, values)
    return values


def build_stencil(nb_ref, cf_ref, code_ref, low_ref, coeff_ref, s_ref):
    points = nb_ref.shape[1]
    high_count = s_ref.shape[1] // LOW
    lane = iota((8, LANES), 1)
    for m in range(points // LANES):
        part = slice(m * LANES, (m + 1) * LANES)
        rows = slice(m * 8, (m + 1) * 8)
        index = regroup(nb_ref[:, part])
        code_ref[rows, :] = (lax.div(index, LOW) * GROUP + (lane & (GROUP - 1))).astype(F32)
        low_ref[rows, :] = (index & (LOW - 1)).astype(F32)
        coeff_ref[rows, :] = regroup(cf_ref[:, part])
    high_rows = iota((high_count * GROUP, LANES), 0).astype(F32).astype(BF16)
    low_rows = iota((LOW, LANES), 0).astype(F32).astype(BF16)
    one, zero = jnp.ones((), BF16), jnp.zeros((), BF16)
    for g in range(points // GROUP):
        code, low_row, coeff = (ref[g : g + 1, :].astype(BF16) for ref in (code_ref, low_ref, coeff_ref))
        high = jnp.where(high_rows == code, one, zero)
        low = jnp.where(low_rows == low_row, coeff, zero)
        out = dot(high, low, 1, 1).astype(BF16)
        for h in range(high_count):
            s_ref[g * GROUP : (g + 1) * GROUP, h * LOW : (h + 1) * LOW] = out[
                h * GROUP : (h + 1) * GROUP
            ]


def one_hot_columns(row, height):
    return jnp.where(iota((height, LANES), 0) == row, 1.0, 0.0).astype(BF16)


def one_hot_rows(row, width):
    column = jnp.broadcast_to(row.astype(F32), (LANES, LANES)).T
    lane = iota((LANES, LANES), 1).astype(F32)
    parts = [jnp.where(column == lane + float(c * LANES), 1.0, 0.0) for c in range(width // LANES)]
    return jnp.concatenate([part.astype(BF16) for part in parts], axis=1)


def send_selector(send_ref, slot, direction, points):
    half = send_ref.shape[1]
    first = SLOTS[slot] // 2 * 2
    columns = []
    for h in range(half // LANES):
        lanes = slice(h * LANES, (h + 1) * LANES)
        row = jnp.where(
            direction == first, send_ref[first : first + 1, lanes], send_ref[first + 1 : first + 2, lanes]
        )
        columns.append(one_hot_columns(row, points))
    return jnp.concatenate(columns, axis=1)


def halo_part(ref, rows, direction, points, half):
    return ref[rows, pl.ds(pl.multiple_of(points + (direction ^ 1) * half, half), half)]


def adjoint_kernel(
    live_ref, field_hbm, send_hbm, nb_hbm, cf_hbm, vert_hbm, w_hbm, map_hbm, cot_hbm,
    sent0, sent1, sent2, sent3, s_ref, mbt_ref, field_ref, send_ref, w_ref, mix_ref, map_ref,
    nb_ref, cf_ref, vert_ref, cot_ref,
    code_ref, low_ref, coeff_ref, p_ref, bbt_ref, back_ref, sems,
):
    order = neighbor_order()
    points = field_ref.shape[0]
    half = send_ref.shape[1]
    slots, block = map_ref.shape
    live = live_ref[0, 0]
    pairs = (
        (nb_hbm, nb_ref), (cf_hbm, cf_ref), (map_hbm, map_ref), (w_hbm, w_ref), (cot_hbm, cot_ref),
        (vert_hbm, vert_ref), (send_hbm, send_ref), (field_hbm, field_ref),
    )
    copies = [pltpu.make_async_copy(a, b, sems.at[i]) for i, (a, b) in enumerate(pairs)]
    for copy in copies:
        copy.start()
    copies[0].wait()
    copies[1].wait()
    build_stencil(nb_ref, cf_ref, code_ref, low_ref, coeff_ref, s_ref)
    for copy in copies[2:]:
        copy.wait()
    for j in range(slots):
        rows = slice(j * block, (j + 1) * block)
        p_ref[rows, :] = one_hot_rows(map_ref[j : j + 1, :], points)
        result = dot(cot_ref[rows, :], w_ref[j], 0, 0)
        bbt_ref[:, rows] = jnp.where(j < live, result, 0.0).astype(BF16)
    mixing = mixing_matrix(vert_ref[...])
    mix_ref[...] = mixing.T.astype(BF16)
    for c in range(points // CHUNK):
        cols = slice(c * CHUNK, (c + 1) * CHUNK)
        back_ref[:, cols] = dot(bbt_ref[...], p_ref[:, cols]).astype(BF16)
    mbt_ref[...] = dot(mixing.astype(BF16), back_ref[...]).astype(BF16)
    field_t = field_ref[...].T
    for slot, sent in enumerate((sent0, sent1, sent2, sent3)):
        sent[:half, :] = dot(field_t, send_selector(send_ref, slot, order[slot], points)).T.astype(BF16)
        part = halo_part(s_ref, slice(None), order[slot], points, half)
        sent[half:, :] = dot(mbt_ref[...], part).T.astype(BF16)


def far_neighbor():
    return lax.axis_index("blk") == 0


def early_kernel(*refs):
    pl.when(jnp.logical_not(far_neighbor()))(lambda: local_work(*refs[:7], *refs[8:12], refs[13]))


def late_kernel(*refs):
    pl.when(far_neighbor())(lambda: local_work(*refs[:7], *refs[11:]))


def local_work(
    got0, got1, mbt_ref, s_ref, field_ref, send_ref, map_ref, own_ref, hor_ref, sel_ref, pt_ref, tile_ref
):
    order = neighbor_order()
    points = field_ref.shape[0]
    half = send_ref.shape[1]
    slots, block = map_ref.shape
    for slot in range(4):
        target = tile_ref if slot < 2 else sel_ref
        start = slot % 2 * half
        target[:, start : start + half] = send_selector(send_ref, slot, order[slot], points)
    index = map_ref[...]
    low = (index & (LANES - 1)).astype(F32).astype(BF16)
    high = lax.div(index, LANES)
    row_ids = iota((LANES, LANES), 0).astype(F32).astype(BF16)
    for p in range(points // LANES):
        here = jnp.where(high == p, 1.0, 0.0).astype(BF16)
        for j in range(slots):
            pt_ref[p * LANES : (p + 1) * LANES, j * block : (j + 1) * block] = jnp.where(
                row_ids == low[j : j + 1], here[j : j + 1], jnp.zeros((), BF16)
            )
    for c in range(points // CHUNK):
        rows = slice(c * CHUNK, (c + 1) * CHUNK)
        own = dot(mbt_ref[...], s_ref[:, rows]).T
        own = own + dot(tile_ref[rows, :half], got0[half:, :])
        own_ref[rows, :] = own + dot(tile_ref[rows, half:], got1[half:, :])
        hor = dot(s_ref[rows, :points], field_ref[...])
        hor = hor + dot(halo_part(s_ref, rows, order[0], points, half), got0[:half, :])
        hor_ref[rows, :] = hor + dot(halo_part(s_ref, rows, order[1], points, half), got1[:half, :])


def forward_kernel(
    live_ref, got2, got3, s_ref, pt_ref, w_ref, mix_ref, own_ref, hor_ref, sel_ref,
    grid_hbm, grad_hbm,
    hb_ref, conv_ref, src_ref, grid_ref, grad_ref, sems,
):
    order = neighbor_order()
    points = hor_ref.shape[0]
    half = got2.shape[0] // 2
    slots, block = w_ref.shape[0], w_ref.shape[1]
    live = live_ref[0, 0]
    for c in range(points // CHUNK):
        rows = slice(c * CHUNK, (c + 1) * CHUNK)
        hor = hor_ref[rows, :] + dot(halo_part(s_ref, rows, order[2], points, half), got2[:half, :])
        hor = hor + dot(halo_part(s_ref, rows, order[3], points, half), got3[:half, :])
        hb_ref[rows, :] = hor.astype(BF16)
    conv_ref[...] = dot(mix_ref[...], hb_ref[...], 1, 1).astype(BF16)
    for c in range(points // CHUNK):
        rows = slice(c * CHUNK, (c + 1) * CHUNK)
        own = own_ref[rows, :] + dot(sel_ref[rows, :half], got2[half:, :])
        grad_ref[rows, :] = (own + dot(sel_ref[rows, half:], got3[half:, :])).astype(BF16)
    copies = [pltpu.make_async_copy(grad_ref, grad_hbm, sems.at[0])]
    copies[0].start()
    for c in range(slots * block // CHUNK):
        cols = slice(c * CHUNK, (c + 1) * CHUNK)
        src_ref[cols, :] = dot(conv_ref[...], pt_ref[:, cols]).T.astype(BF16)
    quarter = slots // 4
    for j in range(slots):
        rows = slice(j * block, (j + 1) * block)
        result = dot(w_ref[j], src_ref[rows, :])
        grid_ref[rows, :] = jnp.where(j < live, result, 0.0).astype(BF16)
        if j % quarter == quarter - 1:
            part = pl.ds((j + 1 - quarter) * block, quarter * block)
            copies.append(pltpu.make_async_copy(grid_ref.at[part], grid_hbm.at[part], sems.at[len(copies)]))
            copies[-1].start()
    for copy in copies:
        copy.wait()


def exchange(value, axis, first, cycle):
    count = lax.axis_size(axis)
    pairs = [(i, (i + 1) % count) for i in range(first, count, 2)]
    if not cycle:
        pairs = [(a, b) for a, b in pairs if a < b]
    return lax.ppermute(value, axis, pairs + [(b, a) for a, b in pairs])


def shards(field, grid_cotangent, send_rows, neighbors, stencil, vertical, interp_weights, block_map, tally):
    field = field[0, 0]
    cotangent = grid_cotangent[0, 0]
    send = send_rows[0, 0]
    nb = neighbors[0, 0].T
    cf = stencil[0, 0].T
    weights = interp_weights[0, 0]
    mapped = block_map[0, 0]
    vert = vertical.reshape(-1, vertical.shape[-1])
    points, feat = field.shape
    half = send.shape[1]
    width = points + 4 * half
    slots, block = mapped.shape
    vmem = pl.BlockSpec(memory_space=pltpu.VMEM)
    smem = pl.BlockSpec(memory_space=pltpu.SMEM)
    hbm = pl.BlockSpec(memory_space=pltpu.HBM)

    def in_vmem(*values):
        return [pltpu.with_memory_space_constraint(value, pltpu.VMEM) for value in values]

    def in_hbm(*values):
        return [pltpu.with_memory_space_constraint(value, pltpu.HBM) for value in values]

    def cost(flops):
        return pl.CostEstimate(flops=flops, bytes_accessed=10**6, transcendentals=0)

    params = pltpu.CompilerParams(vmem_limit_bytes=VMEM_LIMIT)
    shared = (
        pltpu.VMEM((points, width), BF16),
        pltpu.VMEM((feat, points), BF16),
        pltpu.VMEM(field.shape, BF16),
        pltpu.VMEM(send.shape, I32),
        pltpu.VMEM(weights.shape, BF16),
        pltpu.VMEM((feat, feat), BF16),
        pltpu.VMEM(mapped.shape, I32),
    )
    sent0, sent1, sent2, sent3, s_mat, mbt, field_v, send_v, w_v, mix, map_v = pl.pallas_call(
        adjoint_kernel,
        out_shape=(pltpu.VMEM((2 * half, feat), BF16),) * 4 + shared,
        in_specs=[smem] + [hbm] * 8,
        out_specs=(vmem,) * 11,
        scratch_shapes=[
            pltpu.VMEM(nb.shape, I32),
            pltpu.VMEM(cf.shape, F32),
            pltpu.VMEM(vert.shape, F32),
            pltpu.VMEM(cotangent.shape, BF16),
            pltpu.VMEM((points // GROUP, LANES), F32),
            pltpu.VMEM((points // GROUP, LANES), F32),
            pltpu.VMEM((points // GROUP, LANES), F32),
            pltpu.VMEM((slots * block, points), BF16),
            pltpu.VMEM((feat, slots * block), BF16),
            pltpu.VMEM((feat, points), BF16),
            pltpu.SemaphoreType.DMA((8,)),
        ],
        compiler_params=params,
        cost_estimate=cost(2 * 10**9),
    )(tally, *in_hbm(field, send, nb, cf, vert, weights, mapped, cotangent))
    def trade(slot, sent):
        kind = SLOTS[slot]
        return exchange(sent, ("blk", "tile")[kind // 2], kind % 2, kind < 2)

    got0, got1, got2 = trade(0, sent0), trade(1, sent1), trade(2, sent2)
    local_shapes = (
        pltpu.VMEM((points, feat), F32),
        pltpu.VMEM((points, feat), F32),
        pltpu.VMEM((points, 2 * half), BF16),
        pltpu.VMEM((points, slots * block), BF16),
    )
    shared = (got0, got1, mbt, s_mat, field_v, send_v, map_v)
    *local, sent3 = pl.pallas_call(
        early_kernel,
        out_shape=local_shapes + (pltpu.VMEM(sent3.shape, BF16),),
        in_specs=[vmem] * 8,
        out_specs=(vmem,) * 5,
        scratch_shapes=[pltpu.VMEM((points, 2 * half), BF16)],
        input_output_aliases={7: 4},
        compiler_params=params,
        cost_estimate=cost(10**9),
    )(*in_vmem(*shared, sent3))
    got3 = trade(3, sent3)
    own, hor, sel, pt_mat = pl.pallas_call(
        late_kernel,
        out_shape=local_shapes,
        in_specs=[vmem] * 11,
        out_specs=(vmem,) * 4,
        scratch_shapes=[pltpu.VMEM((points, 2 * half), BF16)],
        input_output_aliases={7 + i: i for i in range(4)},
        compiler_params=params,
        cost_estimate=cost(10**9),
    )(*in_vmem(*shared, *local))
    grid, grad = pl.pallas_call(
        forward_kernel,
        out_shape=(
            pltpu.HBM((slots * block, feat), BF16),
            pltpu.HBM((points, feat), BF16),
        ),
        in_specs=[smem] + [vmem] * 9,
        out_specs=(hbm, hbm),
        scratch_shapes=[
            pltpu.VMEM((points, feat), BF16),
            pltpu.VMEM((feat, points), BF16),
            pltpu.VMEM((slots * block, feat), BF16),
            pltpu.VMEM((slots * block, feat), BF16),
            pltpu.VMEM((points, feat), BF16),
            pltpu.SemaphoreType.DMA((5,)),
        ],
        compiler_params=params,
        cost_estimate=cost(10**9),
    )(tally, *in_vmem(got2, got3, s_mat, pt_mat, w_v, mix, own, hor, sel))
    return grid[None, None], grad[None, None]


def solution(mesh):
    four = P("blk", "tile", None, None)
    in_specs = (four, four, four, four, four, P(), P("blk", "tile", None, None, None), four, P("blk", "tile"))
    return jax.shard_map(shards, mesh=mesh, in_specs=in_specs, out_specs=(four, four), check_vma=False)
```
